32 devices in a mesh: group: 2 (over y), seq: 16 (over z, x, core).
Axes of the slice: x: 2, y: 2, z: 4, core: 2. Of those that a mesh axis runs over, the one named last changes fastest.
Arguments:
- ssm_inputs: bfloat16 [4096, 8192], P(('group', 'seq')), parts along dimension 0, may hold values from -6 to 6
- gate_inputs: bfloat16 [4096, 8192], P(('group', 'seq')), parts along dimension 0, may hold values from -81 to 81
- write_keys: bfloat16 [4096, 1024], P(('group', 'seq')), parts along dimension 0, may hold values from -6 to 6
- read_queries: bfloat16 [4096, 1024], P(('group', 'seq')), parts along dimension 0, may hold values from -6 to 6
- step_size: float32 [4096, 128], P(('group', 'seq')), parts along dimension 0, may hold values from 0.003 to 0.3
- decay_rate: float32 [128], replicated, may hold values from 1e-06 to 1.6
- skip_gain: float32 [128], replicated, may hold values from 0.5 to 2
- norm_gain: float32 [8192], replicated, may hold values from 0.5 to 1.5
- query_proj: bfloat16 [4096, 4096], P(('group', 'seq')), parts along dimension 0, may hold values from -9 to 9
- key_proj: bfloat16 [4096, 512], P(('group', 'seq')), parts along dimension 0, may hold values from -9 to 9
- value_proj: bfloat16 [4096, 512], P(('group', 'seq')), parts along dimension 0, may hold values from -6 to 6
- row_ids: int32 [4096], P(('group', 'seq')), parts along dimension 0, may hold values from 0 to 31, as said below
- partners: int32 [32, 4], P(('group', 'seq')), parts along dimension 0, may hold values from -1 to 14, as said below
Outputs:
- mixer_out: bfloat16 [4096, 8192], P(('group', 'seq')), parts along dimension 0
- attention_out: bfloat16 [4096, 4096], P(('group', 'seq')), parts along dimension 0
The draws below stay inside these ranges and needn't reach their ends.
There are 2 independent parts, one for each index of `group`. The reference program is written for one: setup_inputs(seed, part) draws one part's arguments, and reference() takes and returns one part's arrays. A program takes and returns all parts, laid end to end along the dimension named above; an argument that names none is the same for every part. Nothing has to cross between parts.
Inputs may be any that keep to these rules, and one draw needn't show every extreme that they name: row_ids starts at 0 and rises by 0 or 1 from one token to the next, ending at 31. Row b of partners lists distinct blocks b - o with 1 <= o <= 7, -1 marking an unused slot; at most 4 slots are used, and in every draw some block uses all 4.
All inputs are finite; a program needn't handle non-finite values.
Results may differ from the reference program's by a relative error of at most 0.0049.
Values may be sent and summed in bfloat16 or wider, within the bound.
A program may use at most 128 MiB of HBM per device.

```python
import math
import jax
import jax.numpy as jnp
from jax import lax

BLOCK = 128
MH = 128
P_SIZE = 64
NG = 8
N = 128
QH = 32
KVH = 4
HD = 128
WIN = 7
MAXP = 4
NBLK = 16
SEQ = 2048


def row_layout(key):
    count = SEQ // 64 - 1
    picks = jax.random.permutation(jax.random.fold_in(key, 11), SEQ - 1)[:count] + 1
    starts = jnp.zeros((SEQ,), jnp.int32).at[picks].set(1)
    return jnp.cumsum(starts).astype(jnp.int32)


def draw_row_ids(key, part):
    return row_layout(key)


def partner_table(key):
    folded = jax.random.fold_in(key, 23)
    order_key, full_key, small_key, last_key = jax.random.split(folded, 4)
    shuffled = jax.vmap(lambda sub_key: jax.random.permutation(sub_key, WIN))(jax.random.split(order_key, NBLK)) + 1
    chosen = shuffled[:, :MAXP]
    last_row = jnp.concatenate([jnp.ones((1,), jnp.int32), (jax.random.permutation(last_key, WIN - 1)[:MAXP - 1] + 2).astype(jnp.int32)])
    chosen = chosen.at[NBLK - 1].set(last_row)
    counts = jnp.where(jax.random.randint(full_key, (NBLK,), 0, 4) == 0, MAXP, jax.random.randint(small_key, (NBLK,), 0, 3))
    counts = jnp.where(jnp.arange(NBLK) == NBLK - 1, MAXP, counts)
    targets = jnp.arange(NBLK)[:, None] - chosen
    usable = (jnp.arange(MAXP)[None, :] < counts[:, None]) & (targets >= 0)
    return jnp.where(usable, targets, -1).astype(jnp.int32)


def draw_partners(key, part):
    return partner_table(key)


def draw_query_proj(key, part):
    drawn = jax.random.truncated_normal(jax.random.fold_in(key, 41), -6.0, 6.0, (SEQ, QH * HD), jnp.float32)
    return drawn.astype(jnp.bfloat16)


def draw_key_proj(key, part):
    drawn = jax.random.truncated_normal(jax.random.fold_in(key, 43), -6.0, 6.0, (SEQ, KVH * HD), jnp.float32)
    return drawn.astype(jnp.bfloat16)


def draw_gate_inputs(key, part):
    column_scale = jnp.exp(jax.random.uniform(jax.random.fold_in(key, 51), (MH * P_SIZE,), jnp.float32, 0.0, math.log(10.0)))
    row_scale = jnp.exp(jax.random.uniform(jax.random.fold_in(key, 52), (SEQ, 1), jnp.float32, -0.7, 0.7))
    center = jax.random.truncated_normal(jax.random.fold_in(key, 53), -4.0, 4.0, (SEQ, MH * P_SIZE), jnp.float32)
    return (center * column_scale[None, :] * row_scale).astype(jnp.bfloat16)


def draw_step_size(key, part):
    head_base = jnp.exp(jax.random.uniform(jax.random.fold_in(key, 61), (MH,), jnp.float32, math.log(0.01), math.log(0.1)))
    block_factor = jnp.exp(jax.random.uniform(jax.random.fold_in(key, 62), (NBLK, MH), jnp.float32, -0.5, 0.5))
    token_factor = jnp.exp(jax.random.uniform(jax.random.fold_in(key, 63), (SEQ, MH), jnp.float32, -0.5, 0.5))
    return head_base[None, :] * jnp.repeat(block_factor, BLOCK, axis=0) * token_factor


def draw_decay_rate(key, part):
    exponent = jax.random.uniform(jax.random.fold_in(key, 71), (MH,), jnp.float32, -5.5, 0.2)
    return jnp.exp(exponent * math.log(10.0))


def block_levels(stream_key, shape, shards, least, top_value):
    def one(dim, blocks):
        heights = jax.random.uniform(jax.random.fold_in(jax.random.fold_in(stream_key, 6), dim), (blocks,), jnp.float32, least / len(shards), top_value / len(shards))
        return jnp.repeat(jnp.exp(heights), shape[dim] // blocks).reshape((-1,) + (1,) * (len(shape) - dim - 1))

    factor_of = one(*shards[0])
    for cut in shards[1:]:
        factor_of = factor_of * one(*cut)
    return factor_of


def normal_values(stream_key, dims, scale, most, cuts=(), kind=jnp.bfloat16):
    values = jax.random.normal(stream_key, dims, jnp.float32) * scale
    if len(cuts) > 0:
        values = block_levels(stream_key, dims, cuts, -0.22, 0.18) * values
    return jnp.clip(values, min=-most, max=most).astype(kind)


def setup_inputs(seed: int = 0, part: int = 0) -> dict:
    arg_keys = jax.random.split(jax.random.key(seed), 14)
    part_keys = jax.random.split(jax.random.fold_in(arg_keys[13], part), 14)
    ssm_inputs = normal_values(part_keys[0], (SEQ, MH * P_SIZE), 1.0, 6.0, ((0, 16),))
    gate_inputs = draw_gate_inputs(jax.random.fold_in(jax.random.fold_in(arg_keys[13], part), 71), part)
    write_keys = normal_values(part_keys[2], (SEQ, NG * N), 1.0, 6.0, ((0, 16),))
    read_queries = normal_values(part_keys[3], (SEQ, NG * N), 1.0, 6.0, ((0, 16),))
    step_size = draw_step_size(jax.random.fold_in(jax.random.fold_in(arg_keys[13], part), 71), part)
    decay_rate = draw_decay_rate(jax.random.fold_in(arg_keys[13], 71), part)
    skip_gain = jnp.clip(jax.random.uniform(arg_keys[6], (MH,), jnp.float32, 0.5, 2.0), 0.5, 2.0)
    norm_gain = jnp.clip(1.0 + 0.1 * jax.random.normal(arg_keys[7], (MH * P_SIZE,), jnp.float32), 0.5, 1.5)
    query_proj = draw_query_proj(jax.random.fold_in(jax.random.fold_in(arg_keys[13], part), 71), part)
    key_proj = draw_key_proj(jax.random.fold_in(jax.random.fold_in(arg_keys[13], part), 71), part)
    value_proj = normal_values(part_keys[10], (SEQ, KVH * HD), 1.0, 6.0, ((0, 16),))
    row_ids = draw_row_ids(jax.random.fold_in(jax.random.fold_in(arg_keys[13], part), 71), part)
    partners = draw_partners(jax.random.fold_in(jax.random.fold_in(arg_keys[13], part), 71), part)
    return {"ssm_inputs": ssm_inputs, "gate_inputs": gate_inputs, "write_keys": write_keys, "read_queries": read_queries, "step_size": step_size, "decay_rate": decay_rate, "skip_gain": skip_gain, "norm_gain": norm_gain, "query_proj": query_proj, "key_proj": key_proj, "value_proj": value_proj, "row_ids": row_ids, "partners": partners}


def mamba_block(x_blk, z_blk, b_blk, c_blk, dt_blk, decay_rate, skip_gain, norm_gain, entering):
    length = x_blk.shape[0]
    heads_per = MH // NG
    x_heads = x_blk.reshape(length, MH, P_SIZE)
    log_rate = -decay_rate[None, :] * dt_blk
    running = jnp.cumsum(log_rate, axis=0)
    block_total = running[-1]
    b_groups = b_blk.reshape(length, NG, N)
    c_groups = c_blk.reshape(length, NG, N)
    cb_scores = jnp.einsum('tgn,sgn->gts', c_groups.astype(jnp.float32), b_groups.astype(jnp.float32))
    running_t = running.T
    causal = jnp.arange(length)[:, None] >= jnp.arange(length)[None, :]
    decay_gap = jnp.where(causal[None], running_t[:, :, None] - running_t[:, None, :], -jnp.inf)
    cb_heads = jnp.broadcast_to(cb_scores[:, None], (NG, heads_per, length, length)).reshape(MH, length, length)
    weights = (cb_heads * jnp.exp(decay_gap) * dt_blk.T[:, None, :]).astype(jnp.bfloat16)
    weights = lax.optimization_barrier(weights)
    y_intra = jnp.einsum('hts,shp->thp', weights.astype(jnp.float32), x_heads.astype(jnp.float32))
    scaled = (x_heads.astype(jnp.float32) * (dt_blk * jnp.exp(block_total[None, :] - running))[:, :, None]).astype(jnp.bfloat16)
    scaled = lax.optimization_barrier(scaled)
    block_state = jnp.einsum('sgkp,sgn->gkpn', scaled.reshape(length, NG, heads_per, P_SIZE).astype(jnp.float32), b_groups.astype(jnp.float32)).reshape(MH, P_SIZE, N)
    y_off = jnp.einsum('tgn,gkpn->tgkp', c_groups.astype(jnp.float32), entering.reshape(NG, heads_per, P_SIZE, N), precision=lax.Precision.HIGHEST).reshape(length, MH, P_SIZE)
    y_all = y_intra + jnp.exp(running)[:, :, None] * y_off + skip_gain[None, :, None] * x_heads.astype(jnp.float32)
    gated_out = y_all.reshape(length, MH * P_SIZE) * jax.nn.silu(z_blk.astype(jnp.float32))
    grouped = gated_out.reshape(length, NG, MH * P_SIZE // NG)
    inv_rms = lax.rsqrt(lax.optimization_barrier(jnp.mean(grouped * grouped, axis=2, keepdims=True)) + 1e-05)
    normed = ((grouped * inv_rms).reshape(length, MH * P_SIZE) * norm_gain[None, :]).astype(jnp.bfloat16)
    return (normed, block_state, block_total)

def attend(block_index, query_blk, slot_rows, paired_all, table_rows):
    length = BLOCK
    start_row = (block_index * length).astype(jnp.int32)
    own_kv = lax.dynamic_slice_in_dim(paired_all, start_row, length, 0)
    picked = [lax.dynamic_slice_in_dim(paired_all, (jnp.maximum(slot_rows[slot_index], 0) * length).astype(jnp.int32), length, 0) for slot_index in range(MAXP)]
    keyset = jnp.concatenate([own_kv] + picked, axis=0).reshape((MAXP + 1) * length, 2, KVH, HD).astype(jnp.float32)
    own_rows = lax.dynamic_slice_in_dim(table_rows, start_row, length, 0)
    causal = jnp.arange(length)[:, None] >= jnp.arange(length)[None, :]
    own_mask = causal & (own_rows[:, None] == own_rows[None, :])
    slot_used = slot_rows >= 0
    far_mask = jnp.broadcast_to(jnp.repeat(slot_used, length)[None, :], (length, MAXP * length))
    allowed = jnp.concatenate([own_mask, far_mask], axis=1)
    query_groups = query_blk.reshape(length, KVH, QH // KVH, HD).astype(jnp.float32)
    scores = jnp.einsum('tgkd,jgd->gktj', query_groups, keyset[:, 0]) * (1.0 / math.sqrt(HD))
    masked = jnp.where(allowed, scores, -jnp.inf)
    highest = lax.optimization_barrier(jnp.max(masked, axis=3, keepdims=True))
    exp_terms = jnp.where(allowed, jnp.exp(masked - highest), 0.0)
    totals = lax.optimization_barrier(jnp.sum(exp_terms, axis=3, keepdims=True))
    weights_bf = lax.optimization_barrier(exp_terms.astype(jnp.bfloat16))
    summed = jnp.einsum('gktj,jgd->tgkd', weights_bf.astype(jnp.float32), keyset[:, 1])
    return (summed / jnp.transpose(totals, (2, 0, 1, 3))).reshape(length, QH * HD).astype(jnp.bfloat16)

def reference(ssm_inputs, gate_inputs, write_keys, read_queries, step_size, decay_rate, skip_gain, norm_gain, query_proj, key_proj, value_proj, row_ids, partners):

    def to_blocks(array):
        return array.reshape((NBLK, BLOCK) + array.shape[1:])

    def advance(entering, pieces):
        x_blk, z_blk, b_blk, c_blk, dt_blk = pieces
        normed, block_state, block_total = mamba_block(x_blk, z_blk, b_blk, c_blk, dt_blk, decay_rate, skip_gain, norm_gain, entering)
        return (jnp.exp(block_total)[:, None, None] * entering + block_state, normed)
    start_state = jnp.zeros((MH, P_SIZE, N), jnp.float32)
    _, mixer_blocks = lax.scan(advance, start_state, (to_blocks(ssm_inputs), to_blocks(gate_inputs), to_blocks(write_keys), to_blocks(read_queries), to_blocks(step_size)))
    mixer_out = mixer_blocks.reshape(SEQ, MH * P_SIZE)
    paired_all = jnp.stack([key_proj, value_proj], axis=1)

    def one_block(items):
        block_index, query_blk, slot_rows = items
        return attend(block_index, query_blk, slot_rows, paired_all, row_ids)
    attended = lax.map(one_block, (jnp.arange(NBLK, dtype=jnp.int32), query_proj.reshape(NBLK, BLOCK, QH * HD), partners))
    return (mixer_out, attended.reshape(SEQ, QH * HD))
```

```python
import functools
import math

import jax
import jax.numpy as jnp
from jax import lax
from jax.experimental import pallas as pl
from jax.experimental.pallas import tpu as pltpu
from jax.sharding import PartitionSpec as P

MH = 128
P_SIZE = 64
NG = 8
N = 128
QH = 32
KVH = 4
HD = 128
WIN = 7
MAXP = 4
L = 128
HC = 8
NC = MH // HC
CW = HC * P_SIZE
UNITS = 16
UH = QH // UNITS
MESH = pl.DeviceIdType.MESH
F32 = jnp.float32
BF16 = jnp.bfloat16


def first_slot(b):
    return (b * 3) // 2


def expand(v):
    rows = v.shape[0]
    low = lax.broadcasted_iota(jnp.int32, (rows, 128), 1) < P_SIZE
    return jnp.concatenate(
        [
            jnp.where(
                low,
                jnp.broadcast_to(v[:, j : j + 1], (rows, 128)),
                jnp.broadcast_to(v[:, j + 1 : j + 2], (rows, 128)),
            )
            for j in range(0, HC, 2)
        ],
        axis=1,
    )


def kernel(
    nblk, x, z, bk, cq, dt, decay, skip, gain, q, k, v, rid_c, rid_r, partners,
    mix, att,
    state, yint, run_t, dt_t, rcol, scol, ecol, recv, send, kvbuf, own_bias,
    e_send, e_recv, kv_send, kv_recv,
):
    b = lax.axis_index("seq")
    grp = lax.axis_index("group")
    has_next = b + 1 < nblk
    has_prev = b > 0
    barrier = pltpu.get_barrier_semaphore()

    @pl.when(has_next)
    def _():
        pl.semaphore_signal(barrier, inc=1, device_id=(grp, b + 1), device_id_type=MESH)

    @pl.when(has_prev)
    def _():
        pl.semaphore_signal(barrier, inc=1, device_id=(grp, b - 1), device_id_type=MESH)

    row = lax.broadcasted_iota(jnp.int32, (L, L), 0)
    col = lax.broadcasted_iota(jnp.int32, (L, L), 1)
    causal = row >= col
    low = col < P_SIZE

    kvbuf[0, :, : KVH * HD] = k[...]
    kvbuf[0, :, KVH * HD :] = v[...]
    own_bias[...] = jnp.where(causal & (rid_c[...] == rid_r[...]), 0.0, -1e30)

    step = dt[...]
    running = jnp.dot(
        jnp.where(causal, 1.0, 0.0), -(decay[...] * step),
        precision=lax.Precision.HIGHEST, preferred_element_type=F32,
    )
    factor = step * jnp.exp(running[L - 1 : L, :] - running)
    grown = jnp.exp(running)
    run_t[...] = running.T
    dt_t[...] = step.T
    for c in range(NC):
        rcol[c] = running[:, c * HC : (c + 1) * HC]
        scol[c] = factor[:, c * HC : (c + 1) * HC]
        ecol[c] = grown[:, c * HC : (c + 1) * HC]

    @pl.when(jnp.logical_not(has_prev))
    def _():
        recv[...] = jnp.zeros_like(recv)

    ends = jnp.where(has_next, 0, 1) + jnp.where(has_prev, 0, 1)
    pl.semaphore_wait(barrier, 2 - ends)

    def wide(c):
        return pl.ds(pl.multiple_of(c * CW, CW), CW)

    def group_of(c):
        return pl.ds(pl.multiple_of((c // 2) * N, N), N)

    def kv_copy(r):
        return pltpu.make_async_remote_copy(
            src_ref=kvbuf.at[r - 1], dst_ref=kvbuf.at[r],
            send_sem=kv_send.at[r], recv_sem=kv_recv.at[r],
            device_id=(grp, b + 1), device_id_type=MESH,
        )

    def e_copy(c):
        return pltpu.make_async_remote_copy(
            src_ref=send.at[c], dst_ref=recv.at[c],
            send_sem=e_send.at[c], recv_sem=e_recv.at[c],
            device_id=(grp, b + 1), device_id_type=MESH,
        )

    def relay(r):
        @pl.when((r > 1) & (b >= r - 1))
        def _():
            kv_copy(jnp.maximum(r - 1, 1)).wait_recv()

        @pl.when((r <= WIN) & has_next & (b >= r - 1))
        def _():
            kv_copy(jnp.minimum(r, WIN)).start()

    def make_state(c, carry):
        xs = (x[:, wide(c)].astype(F32) * expand(scol[c])).astype(BF16)
        state[c] = lax.dot_general(
            bk[:, group_of(c)], xs, (((0,), (0,)), ((), ())), preferred_element_type=F32
        )
        return carry

    def forward(c):
        @pl.when(has_prev)
        def _():
            e_copy(c).wait_recv()

        @pl.when(has_next)
        def _():
            last = expand(ecol[c, L - 8 : L, :])[7:8, :]
            send[c] = (last * recv[c].astype(F32) + state[c]).astype(send.dtype)
            e_copy(c).start()

    def intra(c):
        cb = lax.dot_general(
            cq[:, group_of(c)], bk[:, group_of(c)], (((1,), (1,)), ((), ())),
            preferred_element_type=F32,
        )
        cb = jnp.where(causal, cb, 0.0)
        xc = x[:, wide(c)]
        cols = rcol[c]
        rows_r = run_t[pl.ds(pl.multiple_of(c * HC, HC), HC), :]
        rows_d = dt_t[pl.ds(pl.multiple_of(c * HC, HC), HC), :]

        def weight(j):
            gap = jnp.minimum(cols[:, j : j + 1] - rows_r[j : j + 1, :], 0.0)
            return (cb * jnp.exp(gap) * rows_d[j : j + 1, :]).astype(BF16)

        parts = []
        for j in range(0, HC, 2):
            xp = xc[:, j * P_SIZE : j * P_SIZE + 128]
            zero = jnp.zeros_like(xp)
            both = jnp.concatenate([jnp.where(low, xp, zero), jnp.where(low, zero, xp)], axis=0)
            w2 = jnp.concatenate([weight(j), weight(j + 1)], axis=1)
            parts.append(jnp.dot(w2, both, preferred_element_type=F32))
        yint[c] = jnp.concatenate(parts, axis=1) + skip[:, wide(c)] * xc.astype(F32)

    def attend(i):
        kh = (i * UH) // (QH // KVH)
        kcol = pl.ds(pl.multiple_of(kh * HD, HD), HD)
        vcol = pl.ds(pl.multiple_of((KVH + kh) * HD, HD), HD)
        keys = [kvbuf[0, :, kcol]]
        vals = [kvbuf[0, :, vcol]]
        bias = [own_bias[...]]
        for j in range(MAXP):
            p = partners[0, j]
            off = jnp.clip(jnp.where(p >= 0, b - p, 0), 0, WIN)
            keys.append(kvbuf[off, :, kcol])
            vals.append(kvbuf[off, :, vcol])
            bias.append(jnp.full((L, L), jnp.where(p >= 0, 0.0, -1e30), F32))
        keys = jnp.concatenate(keys, axis=0)
        vals = jnp.concatenate(vals, axis=0)
        bias = jnp.concatenate(bias, axis=1)
        for u in range(UH):
            hcol = pl.ds(pl.multiple_of((i * UH + u) * HD, HD), HD)
            s = lax.dot_general(
                q[:, hcol], keys, (((1,), (1,)), ((), ())), preferred_element_type=F32
            )
            s = s * (1.0 / math.sqrt(HD)) + bias
            e = jnp.exp(s - jnp.max(s, axis=1, keepdims=True))
            tot = jnp.sum(e, axis=1, keepdims=True)
            o = jnp.dot(e.astype(BF16), vals, preferred_element_type=F32)
            att[:, hcol] = (o / tot).astype(BF16)

    def finish(g, carry):
        ys = []
        total = None
        for half in range(2):
            c = 2 * g + half
            off = jnp.dot(
                cq[:, group_of(c)], recv[c].astype(BF16), preferred_element_type=F32
            )
            zc = z[:, wide(c)].astype(F32)
            y = (yint[c] + expand(ecol[c]) * off) * (zc / (1.0 + jnp.exp(-zc)))
            ys.append(y)
            part = jnp.sum(y * y, axis=1, keepdims=True)
            total = part if total is None else total + part
        inv = lax.rsqrt(total * (1.0 / (2 * CW)) + 1e-05)
        for half in range(2):
            c = 2 * g + half
            mix[:, wide(c)] = (ys[half] * inv * gain[:, wide(c)]).astype(BF16)
        return carry

    lax.fori_loop(0, NC, make_state, 0)
    begin = first_slot(b)

    def slot(s, carry):
        @pl.when((s % 2 == 0) & (s <= 2 * WIN))
        def _():
            relay(s // 2 + 1)

        c = s - begin

        @pl.when((c >= 0) & (c < NC))
        def _():
            forward(jnp.clip(c, 0, NC - 1))

        @pl.when(s < NC)
        def _():
            intra(jnp.minimum(s, NC - 1))

        @pl.when((s >= NC) & (s < NC + UNITS))
        def _():
            attend(jnp.clip(s - NC, 0, UNITS - 1))

        return carry

    lax.fori_loop(0, max(NC + UNITS, first_slot(nblk - 1) + NC), slot, 0)
    lax.fori_loop(0, NG, finish, 0)

    @pl.when(has_next)
    def _():
        def end_e(c, carry):
            e_copy(c).wait_send()
            return carry

        lax.fori_loop(0, NC, end_e, 0)

        def end_kv(r, carry):
            @pl.when(b >= r - 1)
            def _():
                kv_copy(r).wait_send()

            return carry

        lax.fori_loop(1, WIN + 1, end_kv, 0)


def shards(
    nblk, ssm_inputs, gate_inputs, write_keys, read_queries, step_size, decay_rate,
    skip_gain, norm_gain, query_proj, key_proj, value_proj, row_ids, partners,
):
    link = BF16 if nblk <= 32 else F32
    vmem = pl.BlockSpec(memory_space=pltpu.VMEM)
    return tuple(
        pl.pallas_call(
            functools.partial(kernel, nblk),
            out_shape=(
                jax.ShapeDtypeStruct((L, MH * P_SIZE), BF16),
                jax.ShapeDtypeStruct((L, QH * HD), BF16),
            ),
            in_specs=[vmem] * 13 + [pl.BlockSpec(memory_space=pltpu.SMEM)],
            out_specs=(vmem, vmem),
            scratch_shapes=[
                pltpu.VMEM((NC, N, CW), F32),
                pltpu.VMEM((NC, L, CW), F32),
                pltpu.VMEM((MH, L), F32),
                pltpu.VMEM((MH, L), F32),
                pltpu.VMEM((NC, L, HC), F32),
                pltpu.VMEM((NC, L, HC), F32),
                pltpu.VMEM((NC, L, HC), F32),
                pltpu.VMEM((NC, N, CW), link),
                pltpu.VMEM((NC, N, CW), link),
                pltpu.VMEM((WIN + 1, L, 2 * KVH * HD), BF16),
                pltpu.VMEM((L, L), F32),
                pltpu.SemaphoreType.DMA((NC,)),
                pltpu.SemaphoreType.DMA((NC,)),
                pltpu.SemaphoreType.DMA((WIN + 1,)),
                pltpu.SemaphoreType.DMA((WIN + 1,)),
            ],
            compiler_params=pltpu.CompilerParams(
                collective_id=0, has_side_effects=True, vmem_limit_bytes=52 * 1024 * 1024
            ),
            name="layer",
        )(
            ssm_inputs, gate_inputs, write_keys, read_queries, step_size,
            decay_rate[None, :], jnp.repeat(skip_gain, P_SIZE)[None, :], norm_gain[None, :],
            query_proj, key_proj, value_proj, row_ids[:, None], row_ids[None, :], partners,
        )
    )


def solution(mesh):
    rows = P(("group", "seq"), None)
    in_specs = (
        rows, rows, rows, rows, rows, P(), P(), P(), rows, rows, rows, P(("group", "seq")), rows,
    )
    return jax.shard_map(
        functools.partial(shards, mesh.shape["seq"]),
        mesh=mesh, in_specs=in_specs, out_specs=(rows, rows), check_vma=False,
    )
```

```python
import functools
import math

import jax
import jax.numpy as jnp
from jax import lax
from jax.experimental import pallas as pl
from jax.experimental.pallas import tpu as pltpu
from jax.sharding import PartitionSpec as P

MH = 128
P_SIZE = 64
NG = 8
N = 128
QH = 32
KVH = 4
HD = 128
WIN = 7
MAXP = 4
L = 128
HC = 8
NC = MH // HC
CW = HC * P_SIZE
UNITS = 16
LATEST = NC + UNITS - NC // 2
UH = QH // UNITS
MESH = pl.DeviceIdType.MESH
F32 = jnp.float32
BF16 = jnp.bfloat16


def first_slot(b):
    return jnp.minimum((b * 8) // 5, LATEST)


def expand(v):
    rows = v.shape[0]
    low = lax.broadcasted_iota(jnp.int32, (rows, 128), 1) < P_SIZE
    return jnp.concatenate(
        [
            jnp.where(
                low,
                jnp.broadcast_to(v[:, j : j + 1], (rows, 128)),
                jnp.broadcast_to(v[:, j + 1 : j + 2], (rows, 128)),
            )
            for j in range(0, HC, 2)
        ],
        axis=1,
    )


def kernel(
    nblk, x, z, bk, cq, dt, decay, skip, gain, q, k, v, rid_c, rid_r, partners,
    mix, att,
    state, yint, run_t, dt_t, rcol, scol, ecol, recv, send, kvbuf, own_bias,
    e_send, e_recv, kv_send, kv_recv,
):
    b = lax.axis_index("seq")
    grp = lax.axis_index("group")
    has_next = b + 1 < nblk
    has_prev = b > 0
    barrier = pltpu.get_barrier_semaphore()

    @pl.when(has_next)
    def _():
        pl.semaphore_signal(barrier, inc=1, device_id=(grp, b + 1), device_id_type=MESH)

    @pl.when(has_prev)
    def _():
        pl.semaphore_signal(barrier, inc=1, device_id=(grp, b - 1), device_id_type=MESH)

    row = lax.broadcasted_iota(jnp.int32, (L, L), 0)
    col = lax.broadcasted_iota(jnp.int32, (L, L), 1)
    causal = row >= col
    low = col < P_SIZE

    kvbuf[0, :, : KVH * HD] = k[...]
    kvbuf[0, :, KVH * HD :] = v[...]
    own_bias[...] = jnp.where(causal & (rid_c[...] == rid_r[...]), 0.0, -1e30)

    step = dt[...]
    running = jnp.dot(
        jnp.where(causal, 1.0, 0.0), -(decay[...] * step),
        precision=lax.Precision.HIGHEST, preferred_element_type=F32,
    )
    factor = step * jnp.exp(running[L - 1 : L, :] - running)
    grown = jnp.exp(running)
    run_t[...] = running.T
    dt_t[...] = step.T
    for c in range(NC):
        rcol[c] = running[:, c * HC : (c + 1) * HC]
        scol[c] = factor[:, c * HC : (c + 1) * HC]
        ecol[c] = grown[:, c * HC : (c + 1) * HC]

    @pl.when(jnp.logical_not(has_prev))
    def _():
        recv[...] = jnp.zeros_like(recv)

    ends = jnp.where(has_next, 0, 1) + jnp.where(has_prev, 0, 1)
    pl.semaphore_wait(barrier, 2 - ends)

    def wide(c):
        return pl.ds(pl.multiple_of(c * CW, CW), CW)

    def group_of(c):
        return pl.ds(pl.multiple_of((c // 2) * N, N), N)

    def kv_copy(r):
        return pltpu.make_async_remote_copy(
            src_ref=kvbuf.at[r - 1], dst_ref=kvbuf.at[r],
            send_sem=kv_send.at[r], recv_sem=kv_recv.at[r],
            device_id=(grp, b + 1), device_id_type=MESH,
        )

    def e_copy(c):
        return pltpu.make_async_remote_copy(
            src_ref=send.at[c], dst_ref=recv.at[c],
            send_sem=e_send.at[c], recv_sem=e_recv.at[c],
            device_id=(grp, b + 1), device_id_type=MESH,
        )

    def relay(r):
        @pl.when((r > 1) & (b >= r - 1))
        def _():
            kv_copy(jnp.maximum(r - 1, 1)).wait_recv()

        @pl.when((r <= WIN) & has_next & (b >= r - 1))
        def _():
            kv_copy(jnp.minimum(r, WIN)).start()

    def make_state(c, carry):
        xs = (x[:, wide(c)].astype(F32) * expand(scol[c])).astype(BF16)
        state[c] = lax.dot_general(
            bk[:, group_of(c)], xs, (((0,), (0,)), ((), ())), preferred_element_type=F32
        )
        return carry

    def forward(c):
        @pl.when(has_prev)
        def _():
            e_copy(c).wait_recv()

        @pl.when(has_next)
        def _():
            last = expand(ecol[c, L - 8 : L, :])[7:8, :]
            send[c] = (last * recv[c].astype(F32) + state[c]).astype(send.dtype)
            e_copy(c).start()

    def intra(c):
        cb = lax.dot_general(
            cq[:, group_of(c)], bk[:, group_of(c)], (((1,), (1,)), ((), ())),
            preferred_element_type=F32,
        )
        cb = jnp.where(causal, cb, 0.0)
        xc = x[:, wide(c)]
        cols = rcol[c]
        rows_r = run_t[pl.ds(pl.multiple_of(c * HC, HC), HC), :]
        rows_d = dt_t[pl.ds(pl.multiple_of(c * HC, HC), HC), :]

        def weight(j):
            gap = jnp.minimum(cols[:, j : j + 1] - rows_r[j : j + 1, :], 0.0)
            return (cb * jnp.exp(gap) * rows_d[j : j + 1, :]).astype(BF16)

        parts = []
        for j in range(0, HC, 2):
            xp = xc[:, j * P_SIZE : j * P_SIZE + 128]
            zero = jnp.zeros_like(xp)
            both = jnp.concatenate([jnp.where(low, xp, zero), jnp.where(low, zero, xp)], axis=0)
            w2 = jnp.concatenate([weight(j), weight(j + 1)], axis=1)
            parts.append(jnp.dot(w2, both, preferred_element_type=F32))
        yint[c] = jnp.concatenate(parts, axis=1) + skip[:, wide(c)] * xc.astype(F32)

    def attend(i):
        kh = (i * UH) // (QH // KVH)
        kcol = pl.ds(pl.multiple_of(kh * HD, HD), HD)
        vcol = pl.ds(pl.multiple_of((KVH + kh) * HD, HD), HD)
        keys = [kvbuf[0, :, kcol]]
        vals = [kvbuf[0, :, vcol]]
        bias = [own_bias[...]]
        for j in range(MAXP):
            p = partners[0, j]
            off = jnp.clip(jnp.where(p >= 0, b - p, 0), 0, WIN)
            keys.append(kvbuf[off, :, kcol])
            vals.append(kvbuf[off, :, vcol])
            bias.append(jnp.full((L, L), jnp.where(p >= 0, 0.0, -1e30), F32))
        keys = jnp.concatenate(keys, axis=0)
        vals = jnp.concatenate(vals, axis=0)
        bias = jnp.concatenate(bias, axis=1)
        for u in range(UH):
            hcol = pl.ds(pl.multiple_of((i * UH + u) * HD, HD), HD)
            s = lax.dot_general(
                q[:, hcol], keys, (((1,), (1,)), ((), ())), preferred_element_type=F32
            )
            s = s * (1.0 / math.sqrt(HD)) + bias
            e = jnp.exp(s - jnp.max(s, axis=1, keepdims=True))
            tot = jnp.sum(e, axis=1, keepdims=True)
            o = jnp.dot(e.astype(BF16), vals, preferred_element_type=F32)
            att[:, hcol] = (o / tot).astype(BF16)

    def finish(g):
        ys = []
        total = None
        for half in range(2):
            c = 2 * g + half
            off = jnp.dot(
                cq[:, group_of(c)], recv[c].astype(BF16), preferred_element_type=F32
            )
            zc = z[:, wide(c)].astype(F32)
            y = (yint[c] + expand(ecol[c]) * off) * (zc / (1.0 + jnp.exp(-zc)))
            ys.append(y)
            part = jnp.sum(y * y, axis=1, keepdims=True)
            total = part if total is None else total + part
        inv = lax.rsqrt(total * (1.0 / (2 * CW)) + 1e-05)
        for half in range(2):
            c = 2 * g + half
            mix[:, wide(c)] = (ys[half] * inv * gain[:, wide(c)]).astype(BF16)

    lax.fori_loop(0, NC, make_state, 0)
    begin = first_slot(b)

    def slot(s, carry):
        @pl.when((s % 2 == 0) & (s <= 2 * WIN))
        def _():
            relay(s // 2 + 1)

        c = s - begin

        @pl.when((c >= 0) & (c < NC))
        def _():
            forward(jnp.clip(c, 0, NC - 1))

        passing = (c >= 0) & (c < NC)
        unit = jnp.where(c < 0, s, jnp.where(passing, begin + c // 2, s - NC // 2))
        works = jnp.logical_not(passing) | (c % 2 == 0)

        @pl.when(works & (unit < NC))
        def _():
            intra(jnp.minimum(unit, NC - 1))

        @pl.when(works & (unit >= NC) & (unit < NC + UNITS))
        def _():
            attend(jnp.clip(unit - NC, 0, UNITS - 1))

        done = s - LATEST - 1

        @pl.when((done >= 0) & (done % 2 == 0))
        def _():
            finish(jnp.clip(done // 2, 0, NG - 1))

        return carry

    lax.fori_loop(0, LATEST + NC, slot, 0)

    @pl.when(has_next)
    def _():
        def end_e(c, carry):
            e_copy(c).wait_send()
            return carry

        lax.fori_loop(0, NC, end_e, 0)

        def end_kv(r, carry):
            @pl.when(b >= r - 1)
            def _():
                kv_copy(r).wait_send()

            return carry

        lax.fori_loop(1, WIN + 1, end_kv, 0)


def shards(
    nblk, ssm_inputs, gate_inputs, write_keys, read_queries, step_size, decay_rate,
    skip_gain, norm_gain, query_proj, key_proj, value_proj, row_ids, partners,
):
    link = BF16 if nblk <= 32 else F32
    vmem = pl.BlockSpec(memory_space=pltpu.VMEM)
    return tuple(
        pl.pallas_call(
            functools.partial(kernel, nblk),
            out_shape=(
                jax.ShapeDtypeStruct((L, MH * P_SIZE), BF16),
                jax.ShapeDtypeStruct((L, QH * HD), BF16),
            ),
            in_specs=[vmem] * 13 + [pl.BlockSpec(memory_space=pltpu.SMEM)],
            out_specs=(vmem, vmem),
            scratch_shapes=[
                pltpu.VMEM((NC, N, CW), F32),
                pltpu.VMEM((NC, L, CW), F32),
                pltpu.VMEM((MH, L), F32),
                pltpu.VMEM((MH, L), F32),
                pltpu.VMEM((NC, L, HC), F32),
                pltpu.VMEM((NC, L, HC), F32),
                pltpu.VMEM((NC, L, HC), F32),
                pltpu.VMEM((NC, N, CW), link),
                pltpu.VMEM((NC, N, CW), link),
                pltpu.VMEM((WIN + 1, L, 2 * KVH * HD), BF16),
                pltpu.VMEM((L, L), F32),
                pltpu.SemaphoreType.DMA((NC,)),
                pltpu.SemaphoreType.DMA((NC,)),
                pltpu.SemaphoreType.DMA((WIN + 1,)),
                pltpu.SemaphoreType.DMA((WIN + 1,)),
            ],
            compiler_params=pltpu.CompilerParams(
                collective_id=0, has_side_effects=True, vmem_limit_bytes=52 * 1024 * 1024
            ),
            name="layer",
        )(
            ssm_inputs, gate_inputs, write_keys, read_queries, step_size,
            decay_rate[None, :], jnp.repeat(skip_gain, P_SIZE)[None, :], norm_gain[None, :],
            query_proj, key_proj, value_proj, row_ids[:, None], row_ids[None, :], partners,
        )
    )


def solution(mesh):
    rows = P(("group", "seq"), None)
    in_specs = (
        rows, rows, rows, rows, rows, P(), P(), P(), rows, rows, rows, P(("group", "seq")), rows,
    )
    return jax.shard_map(
        functools.partial(shards, mesh.shape["seq"]),
        mesh=mesh, in_specs=in_specs, out_specs=(rows, rows), check_vma=False,
    )
```

```python
import functools
import math

import jax
import jax.numpy as jnp
from jax import lax
from jax.experimental import pallas as pl
from jax.experimental.pallas import tpu as pltpu
from jax.sharding import PartitionSpec as P

MH = 128
P_SIZE = 64
NG = 8
N = 128
QH = 32
KVH = 4
HD = 128
WIN = 7
MAXP = 4
L = 128
HC = 8
NC = MH // HC
CW = HC * P_SIZE
UNITS = 16
LATEST = NC + UNITS
UH = QH // UNITS
MESH = pl.DeviceIdType.MESH
F32 = jnp.float32
BF16 = jnp.bfloat16


def first_slot(b):
    return jnp.minimum(2 * b, LATEST)


def expand(v):
    rows = v.shape[0]
    low = lax.broadcasted_iota(jnp.int32, (rows, 128), 1) < P_SIZE
    return jnp.concatenate(
        [
            jnp.where(
                low,
                jnp.broadcast_to(v[:, j : j + 1], (rows, 128)),
                jnp.broadcast_to(v[:, j + 1 : j + 2], (rows, 128)),
            )
            for j in range(0, HC, 2)
        ],
        axis=1,
    )


def kernel(
    nblk, x, z, bk, cq, dt, decay, skip, gain, q, k, v, rid_c, rid_r, partners,
    mix, att,
    state, yint, run_t, dt_t, rcol, scol, ecol, recv, send, kvbuf, own_bias,
    e_send, e_recv, kv_send, kv_recv,
):
    b = lax.axis_index("seq")
    grp = lax.axis_index("group")
    has_next = b + 1 < nblk
    has_prev = b > 0
    barrier = pltpu.get_barrier_semaphore()

    @pl.when(has_next)
    def _():
        pl.semaphore_signal(barrier, inc=1, device_id=(grp, b + 1), device_id_type=MESH)

    @pl.when(has_prev)
    def _():
        pl.semaphore_signal(barrier, inc=1, device_id=(grp, b - 1), device_id_type=MESH)

    row = lax.broadcasted_iota(jnp.int32, (L, L), 0)
    col = lax.broadcasted_iota(jnp.int32, (L, L), 1)
    causal = row >= col
    low = col < P_SIZE

    kvbuf[0, :, : KVH * HD] = k[...]
    kvbuf[0, :, KVH * HD :] = v[...]
    own_bias[...] = jnp.where(causal & (rid_c[...] == rid_r[...]), 0.0, -1e30)

    step = dt[...]
    running = jnp.dot(
        jnp.where(causal, 1.0, 0.0), -(decay[...] * step),
        precision=lax.Precision.HIGHEST, preferred_element_type=F32,
    )
    factor = step * jnp.exp(running[L - 1 : L, :] - running)
    grown = jnp.exp(running)
    run_t[...] = running.T
    dt_t[...] = step.T
    for c in range(NC):
        rcol[c] = running[:, c * HC : (c + 1) * HC]
        scol[c] = factor[:, c * HC : (c + 1) * HC]
        ecol[c] = grown[:, c * HC : (c + 1) * HC]

    @pl.when(jnp.logical_not(has_prev))
    def _():
        recv[...] = jnp.zeros_like(recv)

    ends = jnp.where(has_next, 0, 1) + jnp.where(has_prev, 0, 1)
    pl.semaphore_wait(barrier, 2 - ends)

    def wide(c):
        return pl.ds(pl.multiple_of(c * CW, CW), CW)

    def group_of(c):
        return pl.ds(pl.multiple_of((c // 2) * N, N), N)

    def kv_copy(r):
        return pltpu.make_async_remote_copy(
            src_ref=kvbuf.at[r - 1], dst_ref=kvbuf.at[r],
            send_sem=kv_send.at[r], recv_sem=kv_recv.at[r],
            device_id=(grp, b + 1), device_id_type=MESH,
        )

    def e_copy(c):
        return pltpu.make_async_remote_copy(
            src_ref=send.at[c], dst_ref=recv.at[c],
            send_sem=e_send.at[c], recv_sem=e_recv.at[c],
            device_id=(grp, b + 1), device_id_type=MESH,
        )

    def relay(r):
        @pl.when((r > 1) & (b >= r - 1))
        def _():
            kv_copy(jnp.maximum(r - 1, 1)).wait_recv()

        @pl.when((r <= WIN) & has_next & (b >= r - 1))
        def _():
            kv_copy(jnp.minimum(r, WIN)).start()

    def make_state(c, carry):
        xs = (x[:, wide(c)].astype(F32) * expand(scol[c])).astype(BF16)
        state[c] = lax.dot_general(
            bk[:, group_of(c)], xs, (((0,), (0,)), ((), ())), preferred_element_type=F32
        )
        return carry

    def forward(c):
        @pl.when(has_prev)
        def _():
            e_copy(c).wait_recv()

        @pl.when(has_next)
        def _():
            last = expand(ecol[c, L - 8 : L, :])[7:8, :]
            send[c] = (last * recv[c].astype(F32) + state[c]).astype(send.dtype)
            e_copy(c).start()

    def intra(c):
        cb = lax.dot_general(
            cq[:, group_of(c)], bk[:, group_of(c)], (((1,), (1,)), ((), ())),
            preferred_element_type=F32,
        )
        cb = jnp.where(causal, cb, 0.0)
        xc = x[:, wide(c)]
        cols = rcol[c]
        rows_r = run_t[pl.ds(pl.multiple_of(c * HC, HC), HC), :]
        rows_d = dt_t[pl.ds(pl.multiple_of(c * HC, HC), HC), :]

        def weight(j):
            gap = jnp.minimum(cols[:, j : j + 1] - rows_r[j : j + 1, :], 0.0)
            return (cb * jnp.exp(gap) * rows_d[j : j + 1, :]).astype(BF16)

        parts = []
        for j in range(0, HC, 2):
            xp = xc[:, j * P_SIZE : j * P_SIZE + 128]
            zero = jnp.zeros_like(xp)
            both = jnp.concatenate([jnp.where(low, xp, zero), jnp.where(low, zero, xp)], axis=0)
            w2 = jnp.concatenate([weight(j), weight(j + 1)], axis=1)
            parts.append(jnp.dot(w2, both, preferred_element_type=F32))
        yint[c] = jnp.concatenate(parts, axis=1) + skip[:, wide(c)] * xc.astype(F32)

    def attend(i):
        kh = (i * UH) // (QH // KVH)
        kcol = pl.ds(pl.multiple_of(kh * HD, HD), HD)
        vcol = pl.ds(pl.multiple_of((KVH + kh) * HD, HD), HD)
        keys = [kvbuf[0, :, kcol]]
        vals = [kvbuf[0, :, vcol]]
        bias = [own_bias[...]]
        for j in range(MAXP):
            p = partners[0, j]
            off = jnp.clip(jnp.where(p >= 0, b - p, 0), 0, WIN)
            keys.append(kvbuf[off, :, kcol])
            vals.append(kvbuf[off, :, vcol])
            bias.append(jnp.full((L, L), jnp.where(p >= 0, 0.0, -1e30), F32))
        keys = jnp.concatenate(keys, axis=0)
        vals = jnp.concatenate(vals, axis=0)
        bias = jnp.concatenate(bias, axis=1)
        for u in range(UH):
            hcol = pl.ds(pl.multiple_of((i * UH + u) * HD, HD), HD)
            s = lax.dot_general(
                q[:, hcol], keys, (((1,), (1,)), ((), ())), preferred_element_type=F32
            )
            s = s * (1.0 / math.sqrt(HD)) + bias
            e = jnp.exp(s - jnp.max(s, axis=1, keepdims=True))
            tot = jnp.sum(e, axis=1, keepdims=True)
            o = jnp.dot(e.astype(BF16), vals, preferred_element_type=F32)
            att[:, hcol] = (o / tot).astype(BF16)

    def finish(g):
        ys = []
        total = None
        for half in range(2):
            c = 2 * g + half
            off = jnp.dot(
                cq[:, group_of(c)], recv[c].astype(BF16), preferred_element_type=F32
            )
            zc = z[:, wide(c)].astype(F32)
            y = (yint[c] + expand(ecol[c]) * off) * (zc / (1.0 + jnp.exp(-zc)))
            ys.append(y)
            part = jnp.sum(y * y, axis=1, keepdims=True)
            total = part if total is None else total + part
        inv = lax.rsqrt(total * (1.0 / (2 * CW)) + 1e-05)
        for half in range(2):
            c = 2 * g + half
            mix[:, wide(c)] = (ys[half] * inv * gain[:, wide(c)]).astype(BF16)

    lax.fori_loop(0, NC, make_state, 0)
    begin = first_slot(b)

    def slot(s, carry):
        @pl.when((s % 2 == 0) & (s <= 2 * WIN))
        def _():
            relay(s // 2 + 1)

        c = s - begin

        @pl.when((c >= 0) & (c < NC))
        def _():
            forward(jnp.clip(c, 0, NC - 1))

        passing = (c >= 0) & (c < NC)
        unit = jnp.where(c < 0, s, jnp.where(passing, begin + c // 2, s - NC // 2))
        works = jnp.logical_not(passing) | (c % 2 == 0)

        @pl.when(works & (unit < NC))
        def _():
            intra(jnp.minimum(unit, NC - 1))

        @pl.when(works & (unit >= NC) & (unit < NC + UNITS))
        def _():
            attend(jnp.clip(unit - NC, 0, UNITS - 1))

        done = s - LATEST - 1

        @pl.when((done >= 0) & (done % 2 == 0))
        def _():
            finish(jnp.clip(done // 2, 0, NG - 1))

        return carry

    lax.fori_loop(0, LATEST + NC, slot, 0)

    @pl.when(has_next)
    def _():
        def end_e(c, carry):
            e_copy(c).wait_send()
            return carry

        lax.fori_loop(0, NC, end_e, 0)

        def end_kv(r, carry):
            @pl.when(b >= r - 1)
            def _():
                kv_copy(r).wait_send()

            return carry

        lax.fori_loop(1, WIN + 1, end_kv, 0)


def shards(
    nblk, ssm_inputs, gate_inputs, write_keys, read_queries, step_size, decay_rate,
    skip_gain, norm_gain, query_proj, key_proj, value_proj, row_ids, partners,
):
    link = BF16 if nblk <= 32 else F32
    vmem = pl.BlockSpec(memory_space=pltpu.VMEM)
    return tuple(
        pl.pallas_call(
            functools.partial(kernel, nblk),
            out_shape=(
                jax.ShapeDtypeStruct((L, MH * P_SIZE), BF16),
                jax.ShapeDtypeStruct((L, QH * HD), BF16),
            ),
            in_specs=[vmem] * 13 + [pl.BlockSpec(memory_space=pltpu.SMEM)],
            out_specs=(vmem, vmem),
            scratch_shapes=[
                pltpu.VMEM((NC, N, CW), F32),
                pltpu.VMEM((NC, L, CW), F32),
                pltpu.VMEM((MH, L), F32),
                pltpu.VMEM((MH, L), F32),
                pltpu.VMEM((NC, L, HC), F32),
                pltpu.VMEM((NC, L, HC), F32),
                pltpu.VMEM((NC, L, HC), F32),
                pltpu.VMEM((NC, N, CW), link),
                pltpu.VMEM((NC, N, CW), link),
                pltpu.VMEM((WIN + 1, L, 2 * KVH * HD), BF16),
                pltpu.VMEM((L, L), F32),
                pltpu.SemaphoreType.DMA((NC,)),
                pltpu.SemaphoreType.DMA((NC,)),
                pltpu.SemaphoreType.DMA((WIN + 1,)),
                pltpu.SemaphoreType.DMA((WIN + 1,)),
            ],
            compiler_params=pltpu.CompilerParams(
                collective_id=0, has_side_effects=True, vmem_limit_bytes=52 * 1024 * 1024
            ),
            name="layer",
        )(
            ssm_inputs, gate_inputs, write_keys, read_queries, step_size,
            decay_rate[None, :], jnp.repeat(skip_gain, P_SIZE)[None, :], norm_gain[None, :],
            query_proj, key_proj, value_proj, row_ids[:, None], row_ids[None, :], partners,
        )
    )


def solution(mesh):
    rows = P(("group", "seq"), None)
    in_specs = (
        rows, rows, rows, rows, rows, P(), P(), P(), rows, rows, rows, P(("group", "seq")), rows,
    )
    return jax.shard_map(
        functools.partial(shards, mesh.shape["seq"]),
        mesh=mesh, in_specs=in_specs, out_specs=(rows, rows), check_vma=False,
    )
```

```python
import functools
import math

import jax
import jax.numpy as jnp
from jax import lax
from jax.experimental import pallas as pl
from jax.experimental.pallas import tpu as pltpu
from jax.sharding import PartitionSpec as P

MH = 128
P_SIZE = 64
NG = 8
N = 128
QH = 32
KVH = 4
HD = 128
WIN = 7
MAXP = 4
L = 128
HC = 8
NC = MH // HC
CW = HC * P_SIZE
UNITS = 16
LATEST = NC + UNITS
UH = QH // UNITS
MESH = pl.DeviceIdType.MESH
F32 = jnp.float32
BF16 = jnp.bfloat16


def first_slot(b):
    return jnp.minimum(2 * b, LATEST)


def expand(v):
    rows = v.shape[0]
    low = lax.broadcasted_iota(jnp.int32, (rows, 128), 1) < P_SIZE
    return jnp.concatenate(
        [
            jnp.where(
                low,
                jnp.broadcast_to(v[:, j : j + 1], (rows, 128)),
                jnp.broadcast_to(v[:, j + 1 : j + 2], (rows, 128)),
            )
            for j in range(0, HC, 2)
        ],
        axis=1,
    )


def kernel(
    nblk, x, z, bk, cq, dt, decay, skip, gain, q, k, v, rid_c, rid_r, partners,
    mix, att,
    state, yint, run_t, dt_t, rcol, scol, ecol, recv, send, kvbuf, own_bias,
    e_send, e_recv, kv_send, kv_recv,
):
    b = lax.axis_index("seq")
    grp = lax.axis_index("group")
    has_next = b + 1 < nblk
    has_prev = b > 0
    barrier = pltpu.get_barrier_semaphore()

    @pl.when(has_next)
    def _():
        pl.semaphore_signal(barrier, inc=1, device_id=(grp, b + 1), device_id_type=MESH)

    @pl.when(has_prev)
    def _():
        pl.semaphore_signal(barrier, inc=1, device_id=(grp, b - 1), device_id_type=MESH)

    row = lax.broadcasted_iota(jnp.int32, (L, L), 0)
    col = lax.broadcasted_iota(jnp.int32, (L, L), 1)
    causal = row >= col
    low = col < P_SIZE

    kvbuf[0, :, : KVH * HD] = k[...]
    kvbuf[0, :, KVH * HD :] = v[...]
    own_bias[...] = jnp.where(causal & (rid_c[...] == rid_r[...]), 0.0, -1e30)

    step = dt[...]
    running = jnp.dot(
        jnp.where(causal, 1.0, 0.0), -(decay[...] * step),
        precision=lax.Precision.HIGHEST, preferred_element_type=F32,
    )
    factor = step * jnp.exp(running[L - 1 : L, :] - running)
    grown = jnp.exp(running)
    run_t[...] = running.T
    dt_t[...] = step.T
    for c in range(NC):
        rcol[c] = running[:, c * HC : (c + 1) * HC]
        scol[c] = factor[:, c * HC : (c + 1) * HC]
        ecol[c] = grown[:, c * HC : (c + 1) * HC]

    @pl.when(jnp.logical_not(has_prev))
    def _():
        recv[...] = jnp.zeros_like(recv)

    ends = jnp.where(has_next, 0, 1) + jnp.where(has_prev, 0, 1)
    pl.semaphore_wait(barrier, 2 - ends)

    def wide(c):
        return pl.ds(pl.multiple_of(c * CW, CW), CW)

    def group_of(c):
        return pl.ds(pl.multiple_of((c // 2) * N, N), N)

    def kv_copy(r):
        return pltpu.make_async_remote_copy(
            src_ref=kvbuf.at[r - 1], dst_ref=kvbuf.at[r],
            send_sem=kv_send.at[r], recv_sem=kv_recv.at[r],
            device_id=(grp, b + 1), device_id_type=MESH,
        )

    def e_copy(c):
        return pltpu.make_async_remote_copy(
            src_ref=send.at[c], dst_ref=recv.at[c],
            send_sem=e_send.at[c], recv_sem=e_recv.at[c],
            device_id=(grp, b + 1), device_id_type=MESH,
        )

    def relay(r):
        @pl.when((r > 1) & (b >= r - 1))
        def _():
            kv_copy(jnp.maximum(r - 1, 1)).wait_recv()

        @pl.when((r <= WIN) & has_next & (b >= r - 1))
        def _():
            kv_copy(jnp.minimum(r, WIN)).start()

    def make_state(c, carry):
        xs = (x[:, wide(c)].astype(F32) * expand(scol[c])).astype(BF16)
        state[c] = lax.dot_general(
            bk[:, group_of(c)], xs, (((0,), (0,)), ((), ())), preferred_element_type=F32
        )
        return carry

    def forward(c):
        @pl.when(has_prev)
        def _():
            e_copy(c).wait_recv()

        @pl.when(has_next)
        def _():
            last = expand(ecol[c, L - 8 : L, :])[7:8, :]
            send[c] = (last * recv[c].astype(F32) + state[c]).astype(send.dtype)
            e_copy(c).start()

    def intra(c):
        cb = lax.dot_general(
            cq[:, group_of(c)], bk[:, group_of(c)], (((1,), (1,)), ((), ())),
            preferred_element_type=F32,
        )
        cb = jnp.where(causal, cb, 0.0)
        xc = x[:, wide(c)]
        cols = rcol[c]
        rows_r = run_t[pl.ds(pl.multiple_of(c * HC, HC), HC), :]
        rows_d = dt_t[pl.ds(pl.multiple_of(c * HC, HC), HC), :]

        def weight(j):
            gap = jnp.minimum(cols[:, j : j + 1] - rows_r[j : j + 1, :], 0.0)
            return (cb * jnp.exp(gap) * rows_d[j : j + 1, :]).astype(BF16)

        parts = []
        for j in range(0, HC, 2):
            xp = xc[:, j * P_SIZE : j * P_SIZE + 128]
            zero = jnp.zeros_like(xp)
            both = jnp.concatenate([jnp.where(low, xp, zero), jnp.where(low, zero, xp)], axis=0)
            w2 = jnp.concatenate([weight(j), weight(j + 1)], axis=1)
            parts.append(jnp.dot(w2, both, preferred_element_type=F32))
        yint[c] = jnp.concatenate(parts, axis=1) + skip[:, wide(c)] * xc.astype(F32)

    def attend(i):
        kh = (i * UH) // (QH // KVH)
        kcol = pl.ds(pl.multiple_of(kh * HD, HD), HD)
        vcol = pl.ds(pl.multiple_of((KVH + kh) * HD, HD), HD)
        keys = [kvbuf[0, :, kcol]]
        vals = [kvbuf[0, :, vcol]]
        bias = [own_bias[...]]
        for j in range(MAXP):
            p = partners[0, j]
            off = jnp.clip(jnp.where(p >= 0, b - p, 0), 0, WIN)
            keys.append(kvbuf[off, :, kcol])
            vals.append(kvbuf[off, :, vcol])
            bias.append(jnp.full((L, L), jnp.where(p >= 0, 0.0, -1e30), F32))
        keys = jnp.concatenate(keys, axis=0)
        vals = jnp.concatenate(vals, axis=0)
        bias = jnp.concatenate(bias, axis=1)
        for u in range(UH):
            hcol = pl.ds(pl.multiple_of((i * UH + u) * HD, HD), HD)
            s = lax.dot_general(
                q[:, hcol], keys, (((1,), (1,)), ((), ())), preferred_element_type=F32
            )
            s = s * (1.0 / math.sqrt(HD)) + bias
            e = jnp.exp(s - jnp.max(s, axis=1, keepdims=True))
            tot = jnp.sum(e, axis=1, keepdims=True)
            o = jnp.dot(e.astype(BF16), vals, preferred_element_type=F32)
            att[:, hcol] = (o / tot).astype(BF16)

    def finish(g):
        ys = []
        total = None
        for half in range(2):
            c = 2 * g + half
            off = jnp.dot(
                cq[:, group_of(c)], recv[c].astype(BF16), preferred_element_type=F32
            )
            zc = z[:, wide(c)].astype(F32)
            y = (yint[c] + expand(ecol[c]) * off) * (zc / (1.0 + jnp.exp(-zc)))
            ys.append(y)
            part = jnp.sum(y * y, axis=1, keepdims=True)
            total = part if total is None else total + part
        inv = lax.rsqrt(total * (1.0 / (2 * CW)) + 1e-05)
        for half in range(2):
            c = 2 * g + half
            mix[:, wide(c)] = (ys[half] * inv * gain[:, wide(c)]).astype(BF16)

    lax.fori_loop(0, NC, make_state, 0)
    begin = first_slot(b)

    def slot(s, carry):
        @pl.when((s % 2 == 0) & (s <= 2 * WIN))
        def _():
            relay(s // 2 + 1)

        c = s - begin

        @pl.when((c >= 0) & (c < NC))
        def _():
            forward(jnp.clip(c, 0, NC - 1))

        passing = (c >= 0) & (c < NC)
        unit = jnp.where(c < 0, s, jnp.where(passing, begin + c // 2, s - NC // 2))
        works = jnp.logical_not(passing) | (c % 2 == 0)

        @pl.when(works & (unit < NC))
        def _():
            intra(jnp.minimum(unit, NC - 1))

        @pl.when(works & (unit >= NC) & (unit < NC + UNITS))
        def _():
            attend(jnp.clip(unit - NC, 0, UNITS - 1))

        done = s - LATEST - 1

        @pl.when((done >= 0) & (done % 2 == 0))
        def _():
            finish(jnp.clip(done // 2, 0, NG - 1))

        return carry

    lax.fori_loop(0, LATEST + NC, slot, 0)

    @pl.when(has_next)
    def _():
        def end_e(c, carry):
            e_copy(c).wait_send()
            return carry

        lax.fori_loop(0, NC, end_e, 0)

        def end_kv(r, carry):
            @pl.when(b >= r - 1)
            def _():
                kv_copy(r).wait_send()

            return carry

        lax.fori_loop(1, WIN + 1, end_kv, 0)


def shards(
    nblk, ssm_inputs, gate_inputs, write_keys, read_queries, step_size, decay_rate,
    skip_gain, norm_gain, query_proj, key_proj, value_proj, row_ids, partners,
):
    link = BF16 if nblk <= 32 else F32
    vmem = pl.BlockSpec(memory_space=pltpu.VMEM)
    return tuple(
        pl.pallas_call(
            functools.partial(kernel, nblk),
            out_shape=(
                jax.ShapeDtypeStruct((L, MH * P_SIZE), BF16),
                jax.ShapeDtypeStruct((L, QH * HD), BF16),
            ),
            in_specs=[vmem] * 13 + [pl.BlockSpec(memory_space=pltpu.SMEM)],
            out_specs=(vmem, vmem),
            scratch_shapes=[
                pltpu.VMEM((NC, N, CW), F32),
                pltpu.VMEM((NC, L, CW), F32),
                pltpu.VMEM((MH, L), F32),
                pltpu.VMEM((MH, L), F32),
                pltpu.VMEM((NC, L, HC), F32),
                pltpu.VMEM((NC, L, HC), F32),
                pltpu.VMEM((NC, L, HC), F32),
                pltpu.VMEM((NC, N, CW), link),
                pltpu.VMEM((NC, N, CW), link),
                pltpu.VMEM((WIN + 1, L, 2 * KVH * HD), BF16),
                pltpu.VMEM((L, L), F32),
                pltpu.SemaphoreType.DMA((NC,)),
                pltpu.SemaphoreType.DMA((NC,)),
                pltpu.SemaphoreType.DMA((WIN + 1,)),
                pltpu.SemaphoreType.DMA((WIN + 1,)),
            ],
            compiler_params=pltpu.CompilerParams(
                collective_id=0, has_side_effects=True, vmem_limit_bytes=63 * 1024 * 1024
            ),
            name="layer",
        )(
            ssm_inputs, gate_inputs, write_keys, read_queries, step_size,
            decay_rate[None, :], jnp.repeat(skip_gain, P_SIZE)[None, :], norm_gain[None, :],
            query_proj, key_proj, value_proj, row_ids[:, None], row_ids[None, :], partners,
        )
    )


def solution(mesh):
    rows = P(("group", "seq"), None)
    in_specs = (
        rows, rows, rows, rows, rows, P(), P(), P(), rows, rows, rows, P(("group", "seq")), rows,
    )
    return jax.shard_map(
        functools.partial(shards, mesh.shape["seq"]),
        mesh=mesh, in_specs=in_specs, out_specs=(rows, rows), check_vma=False,
    )
```
